32 devices in a mesh: seq: 8 (over y, x, core), sub: 4 (over z).
Axes of the slice: x: 2, y: 2, z: 4, core: 2. Of those that a mesh axis runs over, the one named last changes fastest.
Arguments:
- activations: bfloat16 [4096, 1024], P(('seq', 'sub')), may hold values from -6 to 6
- conv_weight: bfloat16 [5, 1152, 1024], P(None, 'sub'), may hold values from -1 to 1
- cotangent: bfloat16 [1024, 1152], P('seq', 'sub'), may hold values from -6 to 6
Outputs:
- features: bfloat16 [1024, 1152], P('seq', 'sub')
- input_grad: bfloat16 [4096, 1024], P(('seq', 'sub'))
- weight_grad: float32 [1024, 5, 1152], P('seq', None, 'sub')
The draws below stay inside these ranges and needn't reach their ends.
All inputs are finite; a program needn't handle non-finite values.
Results may differ from the reference program's by a relative error of at most 0.02.
Values may be sent and summed in bfloat16 or wider, within the bound.
A program may use at most 64 MiB of HBM per device.

```python
import math
import jax
import jax.numpy as jnp
from jax import lax

C1 = 1024
C2 = 1152
KW = 5
L1 = 4096
L3 = 1024
N_SUB = 4


def draw_conv_weight(key, part):
    standard_key, roughness_key = jax.random.split(key)
    standard = jax.random.normal(standard_key, (KW, C2, C1), jnp.float32)
    column = jnp.arange(C2).astype(jnp.float32)
    rising = 0.6 + 1.2 * column / C2
    roughness = jnp.exp(jax.random.uniform(roughness_key, (C2,), jnp.float32, -0.35, 0.35))
    scales = (rising * roughness)[None, :, None]
    scaled = standard * scales / math.sqrt(KW * C1)
    return jnp.clip(scaled, -1.0, 1.0).astype(jnp.bfloat16)


def level_of(rng, extent, pieces, least, high):
    gain = 1.0
    for dim, blocks in pieces:
        draws = jax.random.uniform(jax.random.fold_in(jax.random.fold_in(rng, 6), dim), (blocks,), jnp.float32, least / len(pieces), high / len(pieces))
        gain = gain * jnp.repeat(jnp.exp(draws), extent[dim] // blocks).reshape((-1,) + (1,) * (len(extent) - 1 - dim))
    return gain


def scatter_about(stream_key, dims, scale, limit, cuts=(), kind=jnp.bfloat16):
    array = scale * jax.random.normal(stream_key, dims, jnp.float32)
    if cuts:
        array = array * level_of(stream_key, dims, cuts, -0.22, 0.18)
    return jnp.clip(array, -limit, limit).astype(kind)


def setup_inputs(seed: int = 0) -> dict:
    key_list = jax.random.split(jax.random.key(seed), 4)
    return {
        "activations": scatter_about(key_list[0], (L1, C1), 1.0, 6.0, ((0, 32),)),
        "conv_weight": draw_conv_weight(jax.random.fold_in(key_list[3], 71), 0),
        "cotangent": scatter_about(key_list[2], (L3, C2), 1.0, 6.0, ((0, 8), (1, 4))),
    }


EPSILON = 1e-06

def gelu_slope(tensor):
    return 0.5 * (1.0 + jax.scipy.special.erf(tensor * 0.7071067811865476)) + tensor * jnp.exp(-0.5 * tensor * tensor) * 0.3989422804014327

def pool_pairs(tensor):
    half_rows = tensor.shape[0] // 2
    return 0.5 * lax.optimization_barrier(jnp.sum(tensor.reshape(half_rows, 2, tensor.shape[1]), axis=1))

def reference(activations, conv_weight, cotangent):
    tap_count = conv_weight.shape[0]
    x_float = activations.astype(jnp.float32)
    inv_first = lax.rsqrt(lax.optimization_barrier(jnp.mean(x_float * x_float, axis=1, keepdims=True)) + EPSILON)
    normed_first = x_float * inv_first
    pooled = pool_pairs(jax.nn.gelu(normed_first, approximate=False)).astype(jnp.bfloat16)
    seq_half = pooled.shape[0]
    padded = jnp.pad(pooled, ((2, 2), (0, 0)))
    conv_acc = jnp.zeros((seq_half, C2), jnp.float32)
    for offset in range(tap_count):
        conv_acc = conv_acc + lax.dot_general(padded[offset:offset + seq_half], conv_weight[offset], (((1,), (1,)), ((), ())), preferred_element_type=jnp.float32)
    conv_out = conv_acc.astype(jnp.bfloat16)
    y_float = conv_out.astype(jnp.float32)
    inv_second = lax.rsqrt(lax.optimization_barrier(jnp.mean(y_float * y_float, axis=1, keepdims=True)) + EPSILON)
    normed_second = y_float * inv_second
    features = pool_pairs(jax.nn.gelu(normed_second, approximate=False)).astype(jnp.bfloat16)
    upstream = 0.5 * jnp.repeat(cotangent.astype(jnp.float32), 2, axis=0)
    slope_second = upstream * gelu_slope(normed_second)
    inner_second = lax.optimization_barrier(jnp.mean(slope_second * normed_second, axis=1, keepdims=True))
    conv_grad = (inv_second * (slope_second - normed_second * inner_second)).astype(jnp.bfloat16)
    grad_padded = jnp.pad(conv_grad, ((2, 2), (0, 0)))
    group_width = C2 // N_SUB
    pooled_grad = jnp.zeros((seq_half, C1), jnp.float32)
    for group in range(N_SUB):
        lower_col = group * group_width
        upper_col = lower_col + group_width
        partial_sum = jnp.zeros((seq_half, C1), jnp.float32)
        for offset in range(tap_count):
            partial_sum = partial_sum + jnp.dot(grad_padded[4 - offset:4 - offset + seq_half, lower_col:upper_col], conv_weight[offset, lower_col:upper_col, :], preferred_element_type=jnp.float32)
        rounded = lax.optimization_barrier(partial_sum.astype(jnp.bfloat16))
        pooled_grad = pooled_grad + rounded.astype(jnp.float32)
    slope_first = 0.5 * jnp.repeat(pooled_grad, 2, axis=0) * gelu_slope(normed_first)
    inner_first = lax.optimization_barrier(jnp.mean(slope_first * normed_first, axis=1, keepdims=True))
    input_grad = (inv_first * (slope_first - normed_first * inner_first)).astype(jnp.bfloat16)
    weight_parts = [jnp.dot(padded[offset:offset + seq_half].T, conv_grad, preferred_element_type=jnp.float32) for offset in range(tap_count)]
    weight_grad = jnp.stack(weight_parts, axis=1)
    return (features, input_grad, weight_grad)
```

```python
import functools

import jax
import jax.numpy as jnp
from jax import lax
from jax.experimental import pallas as pl
from jax.experimental.pallas import tpu as pltpu
from jax.sharding import PartitionSpec as P

EPSILON = 1e-06


def padded_2(block, sides, width):
    for axis, dim in sides:
        count = lax.axis_size(axis)
        forward = [(i, i + 1) for i in range(count - 1)]
        backward = [(target, source) for source, target in forward]
        low = lax.ppermute(
            lax.slice_in_dim(block, block.shape[dim] - width, None, axis=dim), axis, forward
        )
        high = lax.ppermute(lax.slice_in_dim(block, 0, width, axis=dim), axis, backward)
        block = jnp.concatenate([low, block, high], axis=dim)
    return block


def gelu_slope(tensor):
    return (
        0.5 * (1.0 + jax.scipy.special.erf(tensor * 0.7071067811865476))
        + tensor * jnp.exp(-0.5 * tensor * tensor) * 0.3989422804014327
    )


def pool_pairs(tensor):
    half_rows = tensor.shape[0] // 2
    return 0.5 * jnp.sum(tensor.reshape(half_rows, 2, tensor.shape[1]), axis=1)


def per_device_plain(activations, conv_weight, cotangent):
    tap_count = conv_weight.shape[0]
    in_width = activations.shape[1]
    out_width = conv_weight.shape[1]
    full_out = out_width * lax.axis_size("sub")
    x_float = activations.astype(jnp.float32)
    inv_first = lax.rsqrt(jnp.mean(x_float * x_float, axis=1, keepdims=True) + EPSILON)
    normed_first = x_float * inv_first
    pooled = pool_pairs(jax.nn.gelu(normed_first, approximate=False)).astype(jnp.bfloat16)
    gathered = lax.all_gather(pooled, "sub", axis=0, tiled=True)
    block_rows = gathered.shape[0]
    padded = padded_2(gathered, (("seq", 0),), 2)
    conv_acc = jnp.zeros((block_rows, out_width), jnp.float32)
    for offset in range(tap_count):
        conv_acc = conv_acc + lax.dot_general(
            padded[offset : offset + block_rows],
            conv_weight[offset],
            (((1,), (1,)), ((), ())),
            preferred_element_type=jnp.float32,
        )
    conv_out = conv_acc.astype(jnp.bfloat16)
    y_float = conv_out.astype(jnp.float32)
    square_sum = lax.psum(jnp.sum(y_float * y_float, axis=1), "sub")
    inv_second = lax.rsqrt(square_sum / full_out + EPSILON)[:, None]
    normed_second = y_float * inv_second
    features = pool_pairs(jax.nn.gelu(normed_second, approximate=False)).astype(jnp.bfloat16)
    upstream = 0.5 * jnp.repeat(cotangent.astype(jnp.float32), 2, axis=0)
    slope_second = upstream * gelu_slope(normed_second)
    inner_second = lax.psum(jnp.sum(slope_second * normed_second, axis=1), "sub")
    conv_grad = (
        inv_second * (slope_second - normed_second * (inner_second / full_out)[:, None])
    ).astype(jnp.bfloat16)
    grad_padded = padded_2(conv_grad, (("seq", 0),), 2)
    running = jnp.zeros((block_rows, in_width), jnp.float32)
    for offset in range(tap_count):
        window = lax.dynamic_slice_in_dim(grad_padded, 0 + 4 - offset, block_rows, 0)
        running = running + jnp.dot(window, conv_weight[offset], preferred_element_type=jnp.float32)
    owned = lax.psum_scatter(
        running.astype(jnp.bfloat16), "sub", scatter_dimension=1, tiled=True
    ).astype(jnp.float32)
    pooled_grad = lax.all_to_all(
        owned.astype(jnp.bfloat16), "sub", split_axis=0, concat_axis=1, tiled=True
    ).astype(owned.dtype)
    slope_first = 0.5 * jnp.repeat(pooled_grad, 2, axis=0) * gelu_slope(normed_first)
    inner_first = jnp.mean(slope_first * normed_first, axis=1, keepdims=True)
    input_grad = (inv_first * (slope_first - normed_first * inner_first)).astype(jnp.bfloat16)
    pieces = [
        lax.dot_general(
            padded[offset : offset + block_rows],
            conv_grad,
            (((0,), (0,)), ((), ())),
            preferred_element_type=jnp.float32,
        )
        for offset in range(tap_count)
    ]
    weight_grad = lax.psum_scatter(
        jnp.stack(pieces, axis=1).astype(jnp.bfloat16), "seq", scatter_dimension=0, tiled=True
    ).astype(jnp.float32)
    return (features, input_grad, weight_grad)


PAD = 16
F32 = jnp.float32
BF16 = jnp.bfloat16


def gelu_half(tensor):
    return 0.5 * (1.0 + lax.erf(tensor * 0.7071067811865476))


def bell(tensor):
    return tensor * jnp.exp(-0.5 * tensor * tensor) * 0.3989422804014327


def fits(activations, conv_weight, n_seq, n_sub):
    rows, in_width = activations.shape
    group = rows * n_sub // 4
    return (
        n_seq % 2 == 0
        and in_width % (n_seq * 128) == 0
        and rows % 64 == 0
        and group % 128 == 0
        and conv_weight.shape[0] == 5
        and conv_weight.shape[1] % 16 == 0
        and n_seq * group <= 2048
    )


def kernel(
    n_seq, n_sub,
    x_ref, w_hbm, cot_ref,
    feat_ref, ig_ref, wg_hbm,
    w_ref, xs, n1, s1, p_ref, pa, gw, ga, sums, q_ref, r_ref, acc,
    w_sem, z_send, z_recv, h_send, h_recv, a_send, a_recv, a_loc, e_send, e_recv,
    g_send, g_recv, b_send, b_recv, l_send, l_recv, q_send, q_recv, wg_sem,
):
    me = lax.axis_index("sub")
    s = lax.axis_index("seq")
    rows, in_width = x_ref.shape
    own = rows // 4
    group = own * n_sub
    ow = w_ref.shape[1]
    full = ow * n_sub
    cs = in_width // n_seq
    n_chip = n_seq // 2
    chip, core = s // 2, s % 2
    taps = w_ref.shape[0]

    def sub_id(d):
        return lax.rem(me + d, n_sub)

    def seq_id(d):
        return lax.rem(s + d, n_seq)

    def copy(src, dst, send, recv, **where):
        return pltpu.make_async_remote_copy(
            src_ref=src, dst_ref=dst, send_sem=send, recv_sem=recv,
            device_id=where, device_id_type=pl.DeviceIdType.MESH,
        )

    w_copy = pltpu.make_async_copy(w_hbm, w_ref, w_sem)
    w_copy.start()

    barrier = pltpu.get_barrier_semaphore()
    for d in range(1, n_sub):
        pl.semaphore_signal(barrier, inc=1, device_id={"sub": sub_id(d)}, device_id_type=pl.DeviceIdType.MESH)
    for d in range(1, n_seq):
        pl.semaphore_signal(barrier, inc=1, device_id={"seq": seq_id(d)}, device_id_type=pl.DeviceIdType.MESH)

    lanes = 128
    for c in range(in_width // lanes):
        xs[c] = x_ref[:, c * lanes : (c + 1) * lanes].astype(F32)
    x_rows = [
        jnp.concatenate([xs[c, pl.ds(r, own, stride=4), :] for c in range(in_width // lanes)], axis=1)
        for r in range(4)
    ]
    inv1 = [lax.rsqrt(jnp.mean(v * v, axis=1, keepdims=True) + EPSILON) for v in x_rows]
    mine = pl.ds(pl.multiple_of(PAD + own * me, 16), own)
    for parity in range(2):
        total = None
        for r in (2 * parity, 2 * parity + 1):
            v = x_rows[r] * inv1[r]
            half = gelu_half(v)
            n1[r] = v
            s1[r] = half + bell(v)
            total = v * half if total is None else total + v * half
        p_ref[parity, mine, :] = (0.5 * total).astype(BF16)

    pl.semaphore_wait(barrier, n_sub + n_seq - 2)

    def z_copy(d, owner):
        part = p_ref.at[:, pl.ds(pl.multiple_of(PAD + own * owner, 16), own), :]
        return copy(part, part, z_send.at[d], z_recv.at[d], sub=sub_id(d))

    for d in range(1, n_sub):
        z_copy(d, me).start()
    for side in (0, PAD + n_seq * group):
        pa[:, side : side + PAD, :] = jnp.zeros((2, PAD, cs), BF16)
    for d in range(1, n_sub):
        z_copy(d, sub_id(n_sub - d)).wait_recv()

    def up(ref, d):
        return copy(ref.at[:, group : group + PAD, :], ref.at[:, 0:PAD, :],
                    h_send.at[d, 0], h_recv.at[d, 0], seq=seq_id(1))

    def down(ref, d):
        return copy(ref.at[:, PAD : 2 * PAD, :], ref.at[:, group + PAD : group + 2 * PAD, :],
                    h_send.at[d, 1], h_recv.at[d, 1], seq=seq_id(n_seq - 1))

    def mask_halo(ref):
        low = ref[:, 0:PAD, :]
        ref[:, 0:PAD, :] = jnp.where(s == 0, jnp.zeros_like(low), low)
        high = ref[:, group + PAD : group + 2 * PAD, :]
        ref[:, group + PAD : group + 2 * PAD, :] = jnp.where(s == n_seq - 1, jnp.zeros_like(high), high)

    up(p_ref, 0).start()
    down(p_ref, 0).start()

    def a_part(block):
        return pa.at[:, pl.ds(pl.multiple_of(PAD + group * block, 16), group), :]

    def a_copy(d, slice_of, block):
        columns = pl.ds(pl.multiple_of(cs * slice_of, 128), cs)
        return copy(p_ref.at[:, PAD : PAD + group, columns], a_part(block),
                    a_send.at[d], a_recv.at[d], seq=seq_id(d))

    for d in range(1, n_seq):
        a_copy(d, seq_id(d), s).start()
    local = pltpu.make_async_copy(
        p_ref.at[:, PAD : PAD + group, pl.ds(pl.multiple_of(cs * s, 128), cs)], a_part(s), a_loc)
    local.start()

    up(p_ref, 0).wait_recv()
    down(p_ref, 0).wait_recv()
    mask_halo(p_ref)
    w_copy.wait()

    def shifts(ref_e, ref_o):
        out = {}
        for name, v in (("e", ref_e), ("o", ref_o)):
            for move in (-1, 0, 1):
                out[name, move] = v[PAD + move : PAD + move + group]
        return out

    even_taps = (("e", -1), ("o", -1), ("e", 0), ("o", 0), ("e", 1))
    odd_taps = (("o", -1), ("e", 0), ("o", 0), ("e", 1), ("o", 1))

    win = shifts(p_ref[0], p_ref[1])
    y = None
    for k in range(taps):
        lhs = jnp.concatenate([win[even_taps[k]], win[odd_taps[k]]], axis=0)
        term = lax.dot_general(lhs, w_ref[k], (((1,), (1,)), ((), ())), preferred_element_type=F32)
        y = term if y is None else y + term
    y = y.astype(BF16).astype(F32)

    def reduce_sub(column, turn):
        wide = jnp.broadcast_to(column, (2 * group, 128)).T
        sums[turn, me] = wide[0:8, :]

        def e_copy(d, owner):
            part = sums.at[turn, owner]
            return copy(part, part, e_send.at[turn, d], e_recv.at[turn, d], sub=sub_id(d))

        for d in range(1, n_sub):
            e_copy(d, me).start()
        for d in range(1, n_sub):
            e_copy(d, sub_id(n_sub - d)).wait_recv()
        total = sums[turn, 0]
        for j in range(1, n_sub):
            total = total + sums[turn, j]
        for d in range(1, n_sub):
            e_copy(d, me).wait_send()
        return jnp.concatenate([total] * 16, axis=0).T[:, 0:1]

    square = reduce_sub(jnp.sum(y * y, axis=1, keepdims=True), 0)
    inv2 = lax.rsqrt(square / full + EPSILON)
    v2 = y * inv2
    half = gelu_half(v2)
    gelu2 = v2 * half
    feat_ref[...] = (0.5 * (gelu2[0:group] + gelu2[group:])).astype(BF16)
    cot = 0.5 * cot_ref[...].astype(F32)
    slope = jnp.concatenate([cot, cot], axis=0) * (half + bell(v2))
    inner = reduce_sub(jnp.sum(slope * v2, axis=1, keepdims=True), 1)
    grad = (inv2 * (slope - v2 * (inner / full))).astype(BF16)
    block_s = pl.ds(pl.multiple_of(PAD + group * s, 16), group)
    for parity in range(2):
        part = grad[parity * group : (parity + 1) * group]
        gw[parity, PAD : PAD + group, :] = part
        ga[parity, block_s, :] = part
    up(gw, 1).start()
    down(gw, 1).start()

    def g_part(block):
        return ga.at[:, pl.ds(pl.multiple_of(PAD + group * block, 16), group), :]

    def g_copy(d, block):
        target = 2 * lax.rem(chip + d, n_chip) + core
        return copy(g_part(block), g_part(block), g_send.at[d], g_recv.at[d], seq=target)

    def b_copy(d, block):
        return copy(g_part(block), g_part(block), b_send.at[d], b_recv.at[d], seq=2 * chip + 1 - core)

    b_copy(0, s).start()
    for d in range(1, n_chip):
        g_copy(d, s).start()

    up(gw, 1).wait_recv()
    down(gw, 1).wait_recv()
    mask_halo(gw)

    gwin = shifts(gw[0], gw[1])
    even_back = (("e", 1), ("o", 0), ("e", 0), ("o", -1), ("e", -1))
    odd_back = (("o", 1), ("e", 1), ("o", 0), ("e", 0), ("o", -1))
    lhs = [jnp.concatenate([gwin[even_back[k]], gwin[odd_back[k]]], axis=0) for k in range(taps)]
    n_col = q_send.shape[0]
    width = in_width // n_col

    def q_copy(c, d, to, owner):
        return copy(
            q_ref.at[c, :, pl.ds(pl.multiple_of(own * to, 16), own), :],
            r_ref.at[owner, c],
            q_send.at[c, d], q_recv.at[c, d], sub=sub_id(d))

    for c in range(n_col):
        total = None
        for k in range(taps):
            term = jnp.dot(lhs[k], w_ref[k, :, c * width : (c + 1) * width], preferred_element_type=F32)
            total = term if total is None else total + term
        q_ref[c] = total.astype(BF16).reshape(2, group, width)
        for d in range(1, n_sub):
            q_copy(c, d, sub_id(d), me).start()
        r_ref[me, c] = q_ref[c, :, pl.ds(pl.multiple_of(own * me, 16), own), :]

    for d in range(1, n_seq):
        a_copy(d, s, seq_id(n_seq - d)).wait_recv()
    local.wait()
    acc[...] = jnp.zeros_like(acc)

    def weight_block(block):
        base = pl.ds(pl.multiple_of(group * block, 16), group + 2 * PAD)
        x_win = shifts(pa[0, base, :], pa[1, base, :])
        left = jnp.concatenate(
            [jnp.concatenate([x_win[even_taps[k]], x_win[odd_taps[k]]], axis=0) for k in range(taps)], axis=1)
        rows_b = pl.ds(pl.multiple_of(PAD + group * block, 16), group)
        right = jnp.concatenate([ga[0, rows_b, :], ga[1, rows_b, :]], axis=0)
        acc[...] += lax.dot_general(left, right, (((0,), (0,)), ((), ())), preferred_element_type=F32)

    weight_block(s)

    def first_pass(d, carry):
        block = 2 * lax.rem(chip + n_chip - d, n_chip) + core
        g_copy(d, block).wait_recv()
        b_copy(d, block).start()
        weight_block(block)
        return carry

    def second_pass(d, carry):
        block = 2 * lax.rem(chip + n_chip - d, n_chip) + 1 - core
        b_copy(d, block).wait_recv()
        weight_block(block)
        return carry

    lax.fori_loop(1, n_chip, first_pass, 0)
    lax.fori_loop(0, n_chip, second_pass, 0)
    wg_copy = pltpu.make_async_copy(acc, wg_hbm, wg_sem)
    wg_copy.start()

    pg = [[], []]
    for c in range(n_col):
        for d in range(1, n_sub):
            q_copy(c, d, me, sub_id(n_sub - d)).wait_recv()
        total = r_ref[0, c].astype(F32)
        for j in range(1, n_sub):
            total = total + r_ref[j, c].astype(F32)
        for parity in range(2):
            pg[parity].append(total[parity])
    pg = [jnp.concatenate(part, axis=1) for part in pg]
    for r in range(4):
        v = n1[r]
        slope1 = 0.5 * pg[r // 2] * s1[r]
        m1 = jnp.mean(slope1 * v, axis=1, keepdims=True)
        out = inv1[r] * (slope1 - v * m1)
        for c in range(in_width // lanes):
            xs[c, pl.ds(r, own, stride=4), :] = out[:, c * lanes : (c + 1) * lanes]
    for c in range(in_width // lanes):
        ig_ref[:, c * lanes : (c + 1) * lanes] = xs[c].astype(BF16)

    for d in range(1, n_sub):
        z_copy(d, me).wait_send()
        for c in range(n_col):
            q_copy(c, d, sub_id(d), me).wait_send()
    for d, ref in ((0, p_ref), (1, gw)):
        up(ref, d).wait_send()
        down(ref, d).wait_send()
    for d in range(1, n_seq):
        a_copy(d, seq_id(d), s).wait_send()
    b_copy(0, s).wait_send()
    for d in range(1, n_chip):
        g_copy(d, s).wait_send()
        b_copy(d, 2 * lax.rem(chip + n_chip - d, n_chip) + core).wait_send()
    wg_copy.wait()


def per_device(activations, conv_weight, cotangent):
    n_seq, n_sub = lax.axis_size("seq"), lax.axis_size("sub")
    if not fits(activations, conv_weight, n_seq, n_sub):
        return per_device_plain(activations, conv_weight, cotangent)
    rows, in_width = activations.shape
    taps, ow, _ = conv_weight.shape
    own = rows // 4
    group = own * n_sub
    cs = in_width // n_seq
    n_chip = n_seq // 2
    n_col = 4
    width = in_width // n_col
    dma = pltpu.SemaphoreType.DMA
    vmem = pl.BlockSpec(memory_space=pltpu.VMEM)
    hbm = pl.BlockSpec(memory_space=pl.ANY)
    features, input_grad, weight_grad = pl.pallas_call(
        functools.partial(kernel, n_seq, n_sub),
        out_shape=(
            jax.ShapeDtypeStruct((group, ow), BF16),
            jax.ShapeDtypeStruct((rows, in_width), BF16),
            jax.ShapeDtypeStruct((taps * cs, ow), F32),
        ),
        in_specs=[vmem, hbm, vmem],
        out_specs=(vmem, vmem, hbm),
        scratch_shapes=[
            pltpu.VMEM((taps, ow, in_width), BF16),
            pltpu.VMEM((in_width // 128, rows, 128), F32),
            pltpu.VMEM((4, own, in_width), F32),
            pltpu.VMEM((4, own, in_width), F32),
            pltpu.VMEM((2, group + 2 * PAD, in_width), BF16),
            pltpu.VMEM((2, n_seq * group + 2 * PAD, cs), BF16),
            pltpu.VMEM((2, group + 2 * PAD, ow), BF16),
            pltpu.VMEM((2, n_seq * group + 2 * PAD, ow), BF16),
            pltpu.VMEM((2, n_sub, 8, 2 * group), F32),
            pltpu.VMEM((n_col, 2, group, width), BF16),
            pltpu.VMEM((n_sub, n_col, 2, own, width), BF16),
            pltpu.VMEM((taps * cs, ow), F32),
            dma, dma((n_sub,)), dma((n_sub,)), dma((2, 2)), dma((2, 2)),
            dma((n_seq,)), dma((n_seq,)), dma, dma((2, n_sub)), dma((2, n_sub)),
            dma((n_chip,)), dma((n_chip,)), dma((n_chip,)), dma((n_chip,)),
            dma, dma, dma((n_col, n_sub)), dma((n_col, n_sub)), dma,
        ],
        compiler_params=pltpu.CompilerParams(
            collective_id=0, has_side_effects=True, vmem_limit_bytes=44 * 1024 * 1024
        ),
        cost_estimate=pl.CostEstimate(
            flops=6 * 2 * group * taps * ow * in_width,
            bytes_accessed=2 * taps * ow * in_width,
            transcendentals=2 * rows * in_width,
        ),
    )(activations, conv_weight, cotangent)
    weight_grad = weight_grad.reshape(taps, cs, ow).transpose(1, 0, 2)
    return (features, input_grad, weight_grad)


def solution(mesh):
    return jax.shard_map(
        per_device,
        mesh=mesh,
        in_specs=(P(("seq", "sub"), None), P(None, "sub", None), P("seq", "sub")),
        out_specs=(P("seq", "sub"), P(("seq", "sub"), None), P("seq", None, "sub")),
        check_vma=False,
    )
```

```python
import functools

import jax
import jax.numpy as jnp
from jax import lax
from jax.experimental import pallas as pl
from jax.experimental.pallas import tpu as pltpu
from jax.sharding import PartitionSpec as P

EPSILON = 1e-06


def padded_2(block, sides, width):
    for axis, dim in sides:
        count = lax.axis_size(axis)
        forward = [(i, i + 1) for i in range(count - 1)]
        backward = [(target, source) for source, target in forward]
        low = lax.ppermute(
            lax.slice_in_dim(block, block.shape[dim] - width, None, axis=dim), axis, forward
        )
        high = lax.ppermute(lax.slice_in_dim(block, 0, width, axis=dim), axis, backward)
        block = jnp.concatenate([low, block, high], axis=dim)
    return block


def gelu_slope(tensor):
    return (
        0.5 * (1.0 + jax.scipy.special.erf(tensor * 0.7071067811865476))
        + tensor * jnp.exp(-0.5 * tensor * tensor) * 0.3989422804014327
    )


def pool_pairs(tensor):
    half_rows = tensor.shape[0] // 2
    return 0.5 * jnp.sum(tensor.reshape(half_rows, 2, tensor.shape[1]), axis=1)


def per_device_plain(activations, conv_weight, cotangent):
    tap_count = conv_weight.shape[0]
    in_width = activations.shape[1]
    out_width = conv_weight.shape[1]
    full_out = out_width * lax.axis_size("sub")
    x_float = activations.astype(jnp.float32)
    inv_first = lax.rsqrt(jnp.mean(x_float * x_float, axis=1, keepdims=True) + EPSILON)
    normed_first = x_float * inv_first
    pooled = pool_pairs(jax.nn.gelu(normed_first, approximate=False)).astype(jnp.bfloat16)
    gathered = lax.all_gather(pooled, "sub", axis=0, tiled=True)
    block_rows = gathered.shape[0]
    padded = padded_2(gathered, (("seq", 0),), 2)
    conv_acc = jnp.zeros((block_rows, out_width), jnp.float32)
    for offset in range(tap_count):
        conv_acc = conv_acc + lax.dot_general(
            padded[offset : offset + block_rows],
            conv_weight[offset],
            (((1,), (1,)), ((), ())),
            preferred_element_type=jnp.float32,
        )
    conv_out = conv_acc.astype(jnp.bfloat16)
    y_float = conv_out.astype(jnp.float32)
    square_sum = lax.psum(jnp.sum(y_float * y_float, axis=1), "sub")
    inv_second = lax.rsqrt(square_sum / full_out + EPSILON)[:, None]
    normed_second = y_float * inv_second
    features = pool_pairs(jax.nn.gelu(normed_second, approximate=False)).astype(jnp.bfloat16)
    upstream = 0.5 * jnp.repeat(cotangent.astype(jnp.float32), 2, axis=0)
    slope_second = upstream * gelu_slope(normed_second)
    inner_second = lax.psum(jnp.sum(slope_second * normed_second, axis=1), "sub")
    conv_grad = (
        inv_second * (slope_second - normed_second * (inner_second / full_out)[:, None])
    ).astype(jnp.bfloat16)
    grad_padded = padded_2(conv_grad, (("seq", 0),), 2)
    running = jnp.zeros((block_rows, in_width), jnp.float32)
    for offset in range(tap_count):
        window = lax.dynamic_slice_in_dim(grad_padded, 0 + 4 - offset, block_rows, 0)
        running = running + jnp.dot(window, conv_weight[offset], preferred_element_type=jnp.float32)
    owned = lax.psum_scatter(
        running.astype(jnp.bfloat16), "sub", scatter_dimension=1, tiled=True
    ).astype(jnp.float32)
    pooled_grad = lax.all_to_all(
        owned.astype(jnp.bfloat16), "sub", split_axis=0, concat_axis=1, tiled=True
    ).astype(owned.dtype)
    slope_first = 0.5 * jnp.repeat(pooled_grad, 2, axis=0) * gelu_slope(normed_first)
    inner_first = jnp.mean(slope_first * normed_first, axis=1, keepdims=True)
    input_grad = (inv_first * (slope_first - normed_first * inner_first)).astype(jnp.bfloat16)
    pieces = [
        lax.dot_general(
            padded[offset : offset + block_rows],
            conv_grad,
            (((0,), (0,)), ((), ())),
            preferred_element_type=jnp.float32,
        )
        for offset in range(tap_count)
    ]
    weight_grad = lax.psum_scatter(
        jnp.stack(pieces, axis=1).astype(jnp.bfloat16), "seq", scatter_dimension=0, tiled=True
    ).astype(jnp.float32)
    return (features, input_grad, weight_grad)


PAD = 16
VMEM_BYTES = 60 * 1024 * 1024
F32 = jnp.float32
BF16 = jnp.bfloat16


def gelu_half(tensor):
    return 0.5 * (1.0 + lax.erf(tensor * 0.7071067811865476))


def bell(tensor):
    return tensor * jnp.exp(-0.5 * tensor * tensor) * 0.3989422804014327


def fits(activations, conv_weight, n_seq, n_sub):
    rows, in_width = activations.shape
    group = rows * n_sub // 4
    return (
        n_seq % 2 == 0
        and in_width % (n_seq * 128) == 0
        and rows % 64 == 0
        and group % 128 == 0
        and conv_weight.shape[0] == 5
        and conv_weight.shape[1] % 16 == 0
        and n_seq * group <= 2048
    )


def kernel(
    n_seq, n_sub, taps,
    x_hbm, w_hbm, cot_hbm,
    feat_hbm, ig_hbm, wg_hbm,
    x_ref, w_ref, cot_ref, feat_ref, ig_ref, xs, n1, s1, p_ref, pa, gw, ga, sums, q_ref, r_ref, acc,
    in_sem, out_sem, z_send, z_recv, h_send, h_recv, k_send, k_recv, a_send, a_recv, a_loc, e_send, e_recv,
    g_send, g_recv, b_send, b_recv, q_send, q_recv,
):
    me = lax.axis_index("sub")
    s = lax.axis_index("seq")
    rows, in_width = x_ref.shape
    own = rows // 4
    group = own * n_sub
    ow = w_ref.shape[0] // taps
    full = ow * n_sub
    cs = in_width // n_seq
    n_chip = n_seq // 2
    chip, core = s // 2, s % 2
    n_col = q_send.shape[0]
    width = in_width // n_col

    def sub_id(d):
        return lax.rem(me + d, n_sub)

    def seq_id(d):
        return lax.rem(s + d, n_seq)

    def copy(src, dst, send, recv, **where):
        return pltpu.make_async_remote_copy(
            src_ref=src, dst_ref=dst, send_sem=send, recv_sem=recv,
            device_id=where, device_id_type=pl.DeviceIdType.MESH,
        )

    loads = [
        pltpu.make_async_copy(src, dst, in_sem.at[i])
        for i, (src, dst) in enumerate(((x_hbm, x_ref), (w_hbm, w_ref), (cot_hbm, cot_ref)))
    ]
    for load in loads:
        load.start()

    barrier = pltpu.get_barrier_semaphore()
    for d in range(1, n_sub):
        pl.semaphore_signal(barrier, inc=1, device_id={"sub": sub_id(d)}, device_id_type=pl.DeviceIdType.MESH)
    for d in range(1, n_seq):
        pl.semaphore_signal(barrier, inc=1, device_id={"seq": seq_id(d)}, device_id_type=pl.DeviceIdType.MESH)
    for side in (0, PAD + n_seq * group):
        pa[:, side : side + PAD, :] = jnp.zeros((2, PAD, cs), BF16)
    loads[0].wait()

    lanes = 128
    n_lane = in_width // lanes
    for c in range(n_lane):
        xs[c] = x_ref[:, c * lanes : (c + 1) * lanes].astype(F32)
    x_rows = [
        jnp.concatenate([xs[c, pl.ds(r, own, stride=4), :] for c in range(n_lane)], axis=1)
        for r in range(4)
    ]
    inv1 = [lax.rsqrt(jnp.mean(v * v, axis=1, keepdims=True) + EPSILON) for v in x_rows]
    mine = pl.ds(pl.multiple_of(PAD + own * me, 16), own)
    for parity in range(2):
        total = None
        for r in (2 * parity, 2 * parity + 1):
            v = x_rows[r] * inv1[r]
            half = gelu_half(v)
            n1[r] = v
            s1[r] = half
            total = v * half if total is None else total + v * half
        p_ref[parity, mine, :] = (0.5 * total).astype(BF16)

    pl.semaphore_wait(barrier, n_sub + n_seq - 2)

    def cols(c):
        return slice(c * width, (c + 1) * width)

    def z_copy(c, d, owner):
        part = p_ref.at[:, pl.ds(pl.multiple_of(PAD + own * owner, 16), own), cols(c)]
        return copy(part, part, z_send.at[c, d], z_recv.at[c, d], sub=sub_id(d))

    for c in range(n_col):
        for d in range(1, n_sub):
            z_copy(c, d, me).start()
    for r in range(4):
        s1[r] += bell(n1[r])

    def up(ref, send, recv):
        return copy(ref.at[:, group : group + PAD, :], ref.at[:, 0:PAD, :], send, recv, seq=seq_id(1))

    def down(ref, send, recv):
        return copy(ref.at[:, PAD : 2 * PAD, :], ref.at[:, group + PAD : group + 2 * PAD, :],
                    send, recv, seq=seq_id(n_seq - 1))

    def halo_pooled(c):
        part = p_ref.at[:, :, cols(c)]
        return (up(part, h_send.at[c, 0], h_recv.at[c, 0]), down(part, h_send.at[c, 1], h_recv.at[c, 1]))

    def halo_grad():
        return (up(gw, k_send.at[0], k_recv.at[0]), down(gw, k_send.at[1], k_recv.at[1]))

    def shifts(v_e, v_o):
        return {
            (name, move): v[PAD + move : PAD + move + group]
            for name, v in (("e", v_e), ("o", v_o))
            for move in (-1, 0, 1)
        }

    def edges(v):
        low, middle, high = v[:, 0:PAD], v[:, PAD : PAD + group], v[:, PAD + group :]
        low = jnp.where(s == 0, jnp.zeros_like(low), low)
        high = jnp.where(s == n_seq - 1, jnp.zeros_like(high), high)
        return jnp.concatenate([low, middle, high], axis=1)

    even_taps = (("e", -1), ("o", -1), ("e", 0), ("o", 0), ("e", 1))
    odd_taps = (("o", -1), ("e", 0), ("o", 0), ("e", 1), ("o", 1))

    def tap_windows(win):
        return jnp.concatenate(
            [jnp.concatenate([win[even_taps[k]], win[odd_taps[k]]], axis=0) for k in range(taps)], axis=1)

    def conv_block(c):
        for halo in halo_pooled(c):
            halo.wait_recv()
        v = edges(p_ref[:, :, cols(c)])
        right = tap_windows(shifts(v[0], v[1]))
        left = jnp.concatenate([w_ref[k * ow : (k + 1) * ow, cols(c)] for k in range(taps)], axis=1)
        return lax.dot_general(left, right, (((1,), (1,)), ((), ())), preferred_element_type=F32)

    y = None
    for c in range(n_col):
        for d in range(1, n_sub):
            z_copy(c, d, sub_id(n_sub - d)).wait_recv()
        for halo in halo_pooled(c):
            halo.start()
        if c == 0:
            loads[1].wait()
        else:
            term = conv_block(c - 1)
            y = term if y is None else y + term

    def a_part(block):
        return pa.at[:, pl.ds(pl.multiple_of(PAD + group * block, 16), group), :]

    def a_copy(d, slice_of, block):
        columns = pl.ds(pl.multiple_of(cs * slice_of, 128), cs)
        return copy(p_ref.at[:, PAD : PAD + group, columns], a_part(block),
                    a_send.at[d], a_recv.at[d], seq=seq_id(d))

    for d in range(1, n_seq):
        a_copy(d, seq_id(d), s).start()
    local = pltpu.make_async_copy(
        p_ref.at[:, PAD : PAD + group, pl.ds(pl.multiple_of(cs * s, 128), cs)], a_part(s), a_loc)
    local.start()
    y = y + conv_block(n_col - 1)
    y = y.astype(BF16).astype(F32)

    def e_copy(turn, d, owner):
        part = sums.at[turn, owner]
        return copy(part, part, e_send.at[turn, d], e_recv.at[turn, d], sub=sub_id(d))

    def reduce_start(turn, values):
        sums[turn, me] = jnp.broadcast_to(jnp.sum(values, axis=0, keepdims=True), (8, 2 * group))
        for d in range(1, n_sub):
            e_copy(turn, d, me).start()

    def reduce_end(turn):
        for d in range(1, n_sub):
            e_copy(turn, d, sub_id(n_sub - d)).wait_recv()
        total = sums[turn, 0]
        for j in range(1, n_sub):
            total = total + sums[turn, j]
        return total[0:1, :]

    reduce_start(0, y * y)
    loads[2].wait()
    cot = 0.5 * cot_ref[...].astype(F32)
    inv2 = lax.rsqrt(reduce_end(0) / full + EPSILON)
    v2 = y * inv2
    half = gelu_half(v2)
    slope = jnp.concatenate([cot, cot], axis=1) * (half + bell(v2))
    reduce_start(1, slope * v2)
    gelu2 = v2 * half
    feat_ref[...] = (0.5 * (gelu2[:, 0:group] + gelu2[:, group:])).astype(BF16)
    outs = [
        pltpu.make_async_copy(src, dst, out_sem.at[i])
        for i, (src, dst) in enumerate(((feat_ref, feat_hbm), (ig_ref, ig_hbm), (acc, wg_hbm)))
    ]
    outs[0].start()
    inner = reduce_end(1)
    grad = inv2 * (slope - v2 * (inner / full))
    turned = grad.T.astype(BF16)
    for parity in range(2):
        gw[parity, PAD : PAD + group, :] = turned[parity * group : (parity + 1) * group]
    for halo in halo_grad():
        halo.start()
    ga[s] = grad.astype(BF16)

    def g_copy(d, block):
        target = 2 * lax.rem(chip + d, n_chip) + core
        return copy(ga.at[block], ga.at[block], g_send.at[d], g_recv.at[d], seq=target)

    def b_copy(d, block):
        return copy(ga.at[block], ga.at[block], b_send.at[d], b_recv.at[d], seq=2 * chip + 1 - core)

    b_copy(0, s).start()
    for d in range(1, n_chip):
        g_copy(d, s).start()

    for halo in halo_grad():
        halo.wait_recv()
    v = edges(gw[...])
    win = shifts(v[0], v[1])
    even_back = (("e", 1), ("o", 0), ("e", 0), ("o", -1), ("e", -1))
    odd_back = (("o", 1), ("e", 1), ("o", 0), ("e", 0), ("o", -1))
    left = jnp.concatenate(
        [jnp.concatenate([win[even_back[k]], win[odd_back[k]]], axis=0) for k in range(taps)], axis=1)

    def q_copy(c, d, to, owner):
        return copy(
            q_ref.at[c, :, pl.ds(pl.multiple_of(own * to, 16), own), :],
            r_ref.at[owner, c],
            q_send.at[c, d], q_recv.at[c, d], sub=sub_id(d))

    for c in range(n_col):
        total = jnp.dot(left, w_ref[:, cols(c)], preferred_element_type=F32)
        q_ref[c] = total.astype(BF16).reshape(2, group, width)
        for d in range(1, n_sub):
            q_copy(c, d, sub_id(d), me).start()
        r_ref[me, c] = q_ref[c, :, pl.ds(pl.multiple_of(own * me, 16), own), :]

    for d in range(1, n_seq):
        a_copy(d, s, seq_id(n_seq - d)).wait_recv()
    local.wait()
    acc[...] = jnp.zeros_like(acc)

    def weight_block(block):
        base = pl.ds(pl.multiple_of(group * block, 16), group + 2 * PAD)
        right = tap_windows(shifts(pa[0, base, :], pa[1, base, :]))
        term = jnp.dot(ga[block], right, preferred_element_type=F32)
        for k in range(taps):
            acc[k] += term[:, k * cs : (k + 1) * cs]

    weight_block(s)

    def first_pass(d, carry):
        block = 2 * lax.rem(chip + n_chip - d, n_chip) + core
        g_copy(d, block).wait_recv()
        b_copy(d, block).start()
        weight_block(block)
        return carry

    def second_pass(d, carry):
        block = 2 * lax.rem(chip + n_chip - d, n_chip) + 1 - core
        b_copy(d, block).wait_recv()
        weight_block(block)
        return carry

    lax.fori_loop(1, n_chip, first_pass, 0)
    lax.fori_loop(0, n_chip, second_pass, 0)
    outs[2].start()

    pg = [[], []]
    for c in range(n_col):
        for d in range(1, n_sub):
            q_copy(c, d, me, sub_id(n_sub - d)).wait_recv()
        total = r_ref[0, c].astype(F32)
        for j in range(1, n_sub):
            total = total + r_ref[j, c].astype(F32)
        for parity in range(2):
            pg[parity].append(total[parity])
    pg = [jnp.concatenate(part, axis=1) for part in pg]
    for r in range(4):
        v = n1[r]
        slope1 = 0.5 * pg[r // 2] * s1[r]
        m1 = jnp.mean(slope1 * v, axis=1, keepdims=True)
        out = inv1[r] * (slope1 - v * m1)
        for c in range(n_lane):
            xs[c, pl.ds(r, own, stride=4), :] = out[:, c * lanes : (c + 1) * lanes]
    for c in range(n_lane):
        ig_ref[:, c * lanes : (c + 1) * lanes] = xs[c].astype(BF16)
    outs[1].start()

    for d in range(1, n_sub):
        for c in range(n_col):
            z_copy(c, d, me).wait_send()
            q_copy(c, d, sub_id(d), me).wait_send()
        for turn in range(2):
            e_copy(turn, d, me).wait_send()
    for c in range(n_col):
        for halo in halo_pooled(c):
            halo.wait_send()
    for halo in halo_grad():
        halo.wait_send()
    for d in range(1, n_seq):
        a_copy(d, seq_id(d), s).wait_send()
    b_copy(0, s).wait_send()
    for d in range(1, n_chip):
        g_copy(d, s).wait_send()
        b_copy(d, 2 * lax.rem(chip + n_chip - d, n_chip) + core).wait_send()
    for out in outs:
        out.wait()


def per_device(activations, conv_weight, cotangent):
    n_seq, n_sub = lax.axis_size("seq"), lax.axis_size("sub")
    if not fits(activations, conv_weight, n_seq, n_sub):
        return per_device_plain(activations, conv_weight, cotangent)
    rows, in_width = activations.shape
    taps, ow, _ = conv_weight.shape
    own = rows // 4
    group = own * n_sub
    cs = in_width // n_seq
    n_chip = n_seq // 2
    n_col = 4
    width = in_width // n_col
    dma = pltpu.SemaphoreType.DMA
    hbm = pl.BlockSpec(memory_space=pl.ANY)
    features, input_grad, weight_grad = pl.pallas_call(
        functools.partial(kernel, n_seq, n_sub, taps),
        out_shape=(
            jax.ShapeDtypeStruct((ow, group), BF16),
            jax.ShapeDtypeStruct((rows, in_width), BF16),
            jax.ShapeDtypeStruct((taps, ow, cs), F32),
        ),
        in_specs=[hbm, hbm, hbm],
        out_specs=(hbm, hbm, hbm),
        scratch_shapes=[
            pltpu.VMEM((rows, in_width), BF16),
            pltpu.VMEM((taps * ow, in_width), BF16),
            pltpu.VMEM((ow, group), BF16),
            pltpu.VMEM((ow, group), BF16),
            pltpu.VMEM((rows, in_width), BF16),
            pltpu.VMEM((in_width // 128, rows, 128), F32),
            pltpu.VMEM((4, own, in_width), F32),
            pltpu.VMEM((4, own, in_width), F32),
            pltpu.VMEM((2, group + 2 * PAD, in_width), BF16),
            pltpu.VMEM((2, n_seq * group + 2 * PAD, cs), BF16),
            pltpu.VMEM((2, group + 2 * PAD, ow), BF16),
            pltpu.VMEM((n_seq, ow, 2 * group), BF16),
            pltpu.VMEM((2, n_sub, 8, 2 * group), F32),
            pltpu.VMEM((n_col, 2, group, width), BF16),
            pltpu.VMEM((n_sub, n_col, 2, own, width), BF16),
            pltpu.VMEM((taps, ow, cs), F32),
            dma((3,)), dma((3,)), dma((n_col, n_sub)), dma((n_col, n_sub)),
            dma((n_col, 2)), dma((n_col, 2)), dma((2,)), dma((2,)),
            dma((n_seq,)), dma((n_seq,)), dma, dma((2, n_sub)), dma((2, n_sub)),
            dma((n_chip,)), dma((n_chip,)), dma((n_chip,)), dma((n_chip,)),
            dma((n_col, n_sub)), dma((n_col, n_sub)),
        ],
        compiler_params=pltpu.CompilerParams(
            collective_id=0, has_side_effects=True, vmem_limit_bytes=VMEM_BYTES
        ),
        cost_estimate=pl.CostEstimate(
            flops=6 * 2 * group * taps * ow * in_width,
            bytes_accessed=2 * taps * ow * in_width,
            transcendentals=2 * rows * in_width,
        ),
    )(activations, conv_weight.reshape(taps * ow, in_width), cotangent.T)
    return (features.T, input_grad, weight_grad.transpose(2, 0, 1))


def solution(mesh):
    return jax.shard_map(
        per_device,
        mesh=mesh,
        in_specs=(P(("seq", "sub"), None), P(None, "sub", None), P("seq", "sub")),
        out_specs=(P("seq", "sub"), P(("seq", "sub"), None), P("seq", None, "sub")),
        check_vma=False,
    )
```

```python
import functools

import jax
import jax.numpy as jnp
from jax import lax
from jax.experimental import pallas as pl
from jax.experimental.pallas import tpu as pltpu
from jax.sharding import PartitionSpec as P

EPSILON = 1e-06


def padded_2(block, sides, width):
    for axis, dim in sides:
        count = lax.axis_size(axis)
        forward = [(i, i + 1) for i in range(count - 1)]
        backward = [(target, source) for source, target in forward]
        low = lax.ppermute(
            lax.slice_in_dim(block, block.shape[dim] - width, None, axis=dim), axis, forward
        )
        high = lax.ppermute(lax.slice_in_dim(block, 0, width, axis=dim), axis, backward)
        block = jnp.concatenate([low, block, high], axis=dim)
    return block


def gelu_slope(tensor):
    return (
        0.5 * (1.0 + jax.scipy.special.erf(tensor * 0.7071067811865476))
        + tensor * jnp.exp(-0.5 * tensor * tensor) * 0.3989422804014327
    )


def pool_pairs(tensor):
    half_rows = tensor.shape[0] // 2
    return 0.5 * jnp.sum(tensor.reshape(half_rows, 2, tensor.shape[1]), axis=1)


def per_device_plain(activations, conv_weight, cotangent):
    tap_count = conv_weight.shape[0]
    in_width = activations.shape[1]
    out_width = conv_weight.shape[1]
    full_out = out_width * lax.axis_size("sub")
    x_float = activations.astype(jnp.float32)
    inv_first = lax.rsqrt(jnp.mean(x_float * x_float, axis=1, keepdims=True) + EPSILON)
    normed_first = x_float * inv_first
    pooled = pool_pairs(jax.nn.gelu(normed_first, approximate=False)).astype(jnp.bfloat16)
    gathered = lax.all_gather(pooled, "sub", axis=0, tiled=True)
    block_rows = gathered.shape[0]
    padded = padded_2(gathered, (("seq", 0),), 2)
    conv_acc = jnp.zeros((block_rows, out_width), jnp.float32)
    for offset in range(tap_count):
        conv_acc = conv_acc + lax.dot_general(
            padded[offset : offset + block_rows],
            conv_weight[offset],
            (((1,), (1,)), ((), ())),
            preferred_element_type=jnp.float32,
        )
    conv_out = conv_acc.astype(jnp.bfloat16)
    y_float = conv_out.astype(jnp.float32)
    square_sum = lax.psum(jnp.sum(y_float * y_float, axis=1), "sub")
    inv_second = lax.rsqrt(square_sum / full_out + EPSILON)[:, None]
    normed_second = y_float * inv_second
    features = pool_pairs(jax.nn.gelu(normed_second, approximate=False)).astype(jnp.bfloat16)
    upstream = 0.5 * jnp.repeat(cotangent.astype(jnp.float32), 2, axis=0)
    slope_second = upstream * gelu_slope(normed_second)
    inner_second = lax.psum(jnp.sum(slope_second * normed_second, axis=1), "sub")
    conv_grad = (
        inv_second * (slope_second - normed_second * (inner_second / full_out)[:, None])
    ).astype(jnp.bfloat16)
    grad_padded = padded_2(conv_grad, (("seq", 0),), 2)
    running = jnp.zeros((block_rows, in_width), jnp.float32)
    for offset in range(tap_count):
        window = lax.dynamic_slice_in_dim(grad_padded, 0 + 4 - offset, block_rows, 0)
        running = running + jnp.dot(window, conv_weight[offset], preferred_element_type=jnp.float32)
    owned = lax.psum_scatter(
        running.astype(jnp.bfloat16), "sub", scatter_dimension=1, tiled=True
    ).astype(jnp.float32)
    pooled_grad = lax.all_to_all(
        owned.astype(jnp.bfloat16), "sub", split_axis=0, concat_axis=1, tiled=True
    ).astype(owned.dtype)
    slope_first = 0.5 * jnp.repeat(pooled_grad, 2, axis=0) * gelu_slope(normed_first)
    inner_first = jnp.mean(slope_first * normed_first, axis=1, keepdims=True)
    input_grad = (inv_first * (slope_first - normed_first * inner_first)).astype(jnp.bfloat16)
    pieces = [
        lax.dot_general(
            padded[offset : offset + block_rows],
            conv_grad,
            (((0,), (0,)), ((), ())),
            preferred_element_type=jnp.float32,
        )
        for offset in range(tap_count)
    ]
    weight_grad = lax.psum_scatter(
        jnp.stack(pieces, axis=1).astype(jnp.bfloat16), "seq", scatter_dimension=0, tiled=True
    ).astype(jnp.float32)
    return (features, input_grad, weight_grad)


PAD = 16
VMEM_BYTES = 60 * 1024 * 1024
F32 = jnp.float32
BF16 = jnp.bfloat16


def gelu_half(tensor):
    return 0.5 * (1.0 + lax.erf(tensor * 0.7071067811865476))


def bell(tensor):
    return tensor * jnp.exp(-0.5 * tensor * tensor) * 0.3989422804014327


def fits(activations, conv_weight, n_seq, n_sub):
    rows, in_width = activations.shape
    group = rows * n_sub // 4
    return (
        n_seq % 2 == 0
        and in_width % (n_seq * 128) == 0
        and rows % 64 == 0
        and group % 128 == 0
        and conv_weight.shape[0] == 5
        and conv_weight.shape[1] % 16 == 0
        and n_seq * group <= 2048
    )


def kernel(
    n_seq, n_sub, taps,
    x_hbm, w_hbm, cot_hbm,
    feat_hbm, ig_hbm, wg_hbm,
    x_ref, w_ref, cot_ref, feat_ref, ig_ref, xs, n1, s1, p_ref, pa, gw, ga, sums, q_ref, r_ref, acc,
    in_sem, out_sem, z_send, z_recv, h_send, h_recv, k_send, k_recv, a_send, a_recv, a_loc, e_send, e_recv,
    g_send, g_recv, b_send, b_recv, q_send, q_recv,
):
    me = lax.axis_index("sub")
    s = lax.axis_index("seq")
    rows, in_width = x_ref.shape
    own = rows // 4
    group = own * n_sub
    ow = w_ref.shape[0] // taps
    full = ow * n_sub
    cs = in_width // n_seq
    n_chip = n_seq // 2
    chip, core = s // 2, s % 2
    n_col = q_send.shape[0]
    width = in_width // n_col

    def sub_id(d):
        return lax.rem(me + d, n_sub)

    def seq_id(d):
        return lax.rem(s + d, n_seq)

    def copy(src, dst, send, recv, **where):
        return pltpu.make_async_remote_copy(
            src_ref=src, dst_ref=dst, send_sem=send, recv_sem=recv,
            device_id=where, device_id_type=pl.DeviceIdType.MESH,
        )

    loads = [
        pltpu.make_async_copy(src, dst, in_sem.at[i])
        for i, (src, dst) in enumerate(((x_hbm, x_ref), (w_hbm, w_ref), (cot_hbm, cot_ref)))
    ]
    for load in loads:
        load.start()

    barrier = pltpu.get_barrier_semaphore()
    for d in range(1, n_sub):
        pl.semaphore_signal(barrier, inc=1, device_id={"sub": sub_id(d)}, device_id_type=pl.DeviceIdType.MESH)
    for d in range(1, n_seq):
        pl.semaphore_signal(barrier, inc=1, device_id={"seq": seq_id(d)}, device_id_type=pl.DeviceIdType.MESH)
    for side in (0, PAD + n_seq * group):
        pa[:, side : side + PAD, :] = jnp.zeros((2, PAD, cs), BF16)
    loads[0].wait()

    lanes = 128
    n_lane = in_width // lanes
    for c in range(n_lane):
        xs[c] = x_ref[:, c * lanes : (c + 1) * lanes].astype(F32)
    x_rows = [
        jnp.concatenate([xs[c, pl.ds(r, own, stride=4), :] for c in range(n_lane)], axis=1)
        for r in range(4)
    ]
    inv1 = [lax.rsqrt(jnp.mean(v * v, axis=1, keepdims=True) + EPSILON) for v in x_rows]
    mine = pl.ds(pl.multiple_of(PAD + own * me, 16), own)
    for parity in range(2):
        total = None
        for r in (2 * parity, 2 * parity + 1):
            v = x_rows[r] * inv1[r]
            half = gelu_half(v)
            n1[r] = v
            s1[r] = half
            total = v * half if total is None else total + v * half
        p_ref[parity, mine, :] = (0.5 * total).astype(BF16)

    pl.semaphore_wait(barrier, n_sub + n_seq - 2)

    def cols(c):
        return slice(c * width, (c + 1) * width)

    ways = ((1, n_sub - 1), (-1, 0))

    def z_copy(c, way, t, owner):
        step = ways[way][0]
        part = p_ref.at[:, pl.ds(pl.multiple_of(PAD + own * owner, 16), own), cols(c)]
        target = lax.rem(me + step + n_sub, n_sub)
        return copy(part, part, z_send.at[c, way, t - 1], z_recv.at[c, way, t - 1], sub=target)

    def has(way, t):
        return me >= t if way == 0 else me + t < n_sub

    def z_send_all(t, c, act):
        for way in range(2):
            step, last = ways[way]
            source = me - step * (t - 1)

            @pl.when(jnp.logical_and(has(way, t - 1), me != last))
            def _():
                act(z_copy(c, way, t, source))

    def z_wait(t, c):
        for way in range(2):
            step, last = ways[way]

            @pl.when(has(way, t))
            def _():
                z_copy(c, way, t, me - step * t).wait_recv()

    def z_start(t, c):
        z_send_all(t, c, lambda one: one.start())

    for c in range(n_col):
        z_start(1, c)
    for r in range(4):
        s1[r] += bell(n1[r])

    def up(ref, send, recv):
        return copy(ref.at[:, group : group + PAD, :], ref.at[:, 0:PAD, :], send, recv, seq=seq_id(1))

    def down(ref, send, recv):
        return copy(ref.at[:, PAD : 2 * PAD, :], ref.at[:, group + PAD : group + 2 * PAD, :],
                    send, recv, seq=seq_id(n_seq - 1))

    def halo_pooled(c):
        part = p_ref.at[:, :, cols(c)]
        return (up(part, h_send.at[c, 0], h_recv.at[c, 0]), down(part, h_send.at[c, 1], h_recv.at[c, 1]))

    def halo_grad():
        return (up(gw, k_send.at[0], k_recv.at[0]), down(gw, k_send.at[1], k_recv.at[1]))

    def shifts(v_e, v_o):
        return {
            (name, move): v[PAD + move : PAD + move + group]
            for name, v in (("e", v_e), ("o", v_o))
            for move in (-1, 0, 1)
        }

    def edges(v):
        low, middle, high = v[:, 0:PAD], v[:, PAD : PAD + group], v[:, PAD + group :]
        low = jnp.where(s == 0, jnp.zeros_like(low), low)
        high = jnp.where(s == n_seq - 1, jnp.zeros_like(high), high)
        return jnp.concatenate([low, middle, high], axis=1)

    even_taps = (("e", -1), ("o", -1), ("e", 0), ("o", 0), ("e", 1))
    odd_taps = (("o", -1), ("e", 0), ("o", 0), ("e", 1), ("o", 1))

    def tap_windows(win):
        return jnp.concatenate(
            [jnp.concatenate([win[even_taps[k]], win[odd_taps[k]]], axis=0) for k in range(taps)], axis=1)

    def conv_block(c):
        for halo in halo_pooled(c):
            halo.wait_recv()
        v = edges(p_ref[:, :, cols(c)])
        right = tap_windows(shifts(v[0], v[1]))
        left = jnp.concatenate([w_ref[k * ow : (k + 1) * ow, cols(c)] for k in range(taps)], axis=1)
        return lax.dot_general(left, right, (((1,), (1,)), ((), ())), preferred_element_type=F32)

    y = None
    for t in range(1, n_sub - 1):
        for c in range(n_col):
            z_wait(t, c)
            z_start(t + 1, c)
    for c in range(n_col):
        z_wait(n_sub - 1, c)
        for halo in halo_pooled(c):
            halo.start()
        if c == 0:
            loads[1].wait()
        else:
            term = conv_block(c - 1)
            y = term if y is None else y + term

    def a_part(block):
        return pa.at[:, pl.ds(pl.multiple_of(PAD + group * block, 16), group), :]

    def a_copy(d, slice_of, block):
        columns = pl.ds(pl.multiple_of(cs * slice_of, 128), cs)
        return copy(p_ref.at[:, PAD : PAD + group, columns], a_part(block),
                    a_send.at[d], a_recv.at[d], seq=seq_id(d))

    for d in range(1, n_seq):
        a_copy(d, seq_id(d), s).start()
    local = pltpu.make_async_copy(
        p_ref.at[:, PAD : PAD + group, pl.ds(pl.multiple_of(cs * s, 128), cs)], a_part(s), a_loc)
    local.start()
    y = y + conv_block(n_col - 1)
    y = y.astype(BF16).astype(F32)

    def e_copy(turn, d, owner):
        part = sums.at[turn, owner]
        return copy(part, part, e_send.at[turn, d], e_recv.at[turn, d], sub=sub_id(d))

    def reduce_start(turn, values):
        sums[turn, me] = jnp.broadcast_to(jnp.sum(values, axis=0, keepdims=True), (8, 2 * group))
        for d in range(1, n_sub):
            e_copy(turn, d, me).start()

    def reduce_end(turn):
        for d in range(1, n_sub):
            e_copy(turn, d, sub_id(n_sub - d)).wait_recv()
        total = sums[turn, 0]
        for j in range(1, n_sub):
            total = total + sums[turn, j]
        return total[0:1, :]

    reduce_start(0, y * y)
    loads[2].wait()
    cot = 0.5 * cot_ref[...].astype(F32)
    inv2 = lax.rsqrt(reduce_end(0) / full + EPSILON)
    v2 = y * inv2
    half = gelu_half(v2)
    slope = jnp.concatenate([cot, cot], axis=1) * (half + bell(v2))
    reduce_start(1, slope * v2)
    gelu2 = v2 * half
    feat_ref[...] = (0.5 * (gelu2[:, 0:group] + gelu2[:, group:])).astype(BF16)
    outs = [
        pltpu.make_async_copy(src, dst, out_sem.at[i])
        for i, (src, dst) in enumerate(((feat_ref, feat_hbm), (ig_ref, ig_hbm), (acc, wg_hbm)))
    ]
    outs[0].start()
    inner = reduce_end(1)
    grad = inv2 * (slope - v2 * (inner / full))
    turned = grad.T.astype(BF16)
    for parity in range(2):
        gw[parity, PAD : PAD + group, :] = turned[parity * group : (parity + 1) * group]
    for halo in halo_grad():
        halo.start()
    ga[s] = grad.astype(BF16)

    def g_copy(d, block):
        target = 2 * lax.rem(chip + d, n_chip) + core
        return copy(ga.at[block], ga.at[block], g_send.at[d], g_recv.at[d], seq=target)

    def b_copy(d, block):
        return copy(ga.at[block], ga.at[block], b_send.at[d], b_recv.at[d], seq=2 * chip + 1 - core)

    b_copy(0, s).start()
    for d in range(1, n_chip):
        g_copy(d, s).start()

    for halo in halo_grad():
        halo.wait_recv()
    v = edges(gw[...])
    win = shifts(v[0], v[1])
    even_back = (("e", 1), ("o", 0), ("e", 0), ("o", -1), ("e", -1))
    odd_back = (("o", 1), ("e", 1), ("o", 0), ("e", 0), ("o", -1))
    left = jnp.concatenate(
        [jnp.concatenate([win[even_back[k]], win[odd_back[k]]], axis=0) for k in range(taps)], axis=1)

    def q_copy(c, d, to, owner):
        return copy(
            q_ref.at[c, :, pl.ds(pl.multiple_of(own * to, 16), own), :],
            r_ref.at[owner, c],
            q_send.at[c, d], q_recv.at[c, d], sub=sub_id(d))

    for c in range(n_col):
        total = jnp.dot(left, w_ref[:, cols(c)], preferred_element_type=F32)
        q_ref[c] = total.astype(BF16).reshape(2, group, width)
        for d in range(1, n_sub):
            q_copy(c, d, sub_id(d), me).start()
        r_ref[me, c] = q_ref[c, :, pl.ds(pl.multiple_of(own * me, 16), own), :]

    for d in range(1, n_seq):
        a_copy(d, s, seq_id(n_seq - d)).wait_recv()
    local.wait()
    acc[...] = jnp.zeros_like(acc)

    def weight_block(block):
        base = pl.ds(pl.multiple_of(group * block, 16), group + 2 * PAD)
        right = tap_windows(shifts(pa[0, base, :], pa[1, base, :]))
        term = jnp.dot(ga[block], right, preferred_element_type=F32)
        for k in range(taps):
            acc[k] += term[:, k * cs : (k + 1) * cs]

    weight_block(s)

    def first_pass(d, carry):
        block = 2 * lax.rem(chip + n_chip - d, n_chip) + core
        g_copy(d, block).wait_recv()
        b_copy(d, block).start()
        weight_block(block)
        return carry

    def second_pass(d, carry):
        block = 2 * lax.rem(chip + n_chip - d, n_chip) + 1 - core
        b_copy(d, block).wait_recv()
        weight_block(block)
        return carry

    lax.fori_loop(1, n_chip, first_pass, 0)
    lax.fori_loop(0, n_chip, second_pass, 0)
    outs[2].start()

    pg = [[], []]
    for c in range(n_col):
        for d in range(1, n_sub):
            q_copy(c, d, me, sub_id(n_sub - d)).wait_recv()
        total = r_ref[0, c].astype(F32)
        for j in range(1, n_sub):
            total = total + r_ref[j, c].astype(F32)
        for parity in range(2):
            pg[parity].append(total[parity])
    pg = [jnp.concatenate(part, axis=1) for part in pg]
    for r in range(4):
        v = n1[r]
        slope1 = 0.5 * pg[r // 2] * s1[r]
        m1 = jnp.mean(slope1 * v, axis=1, keepdims=True)
        out = inv1[r] * (slope1 - v * m1)
        for c in range(n_lane):
            xs[c, pl.ds(r, own, stride=4), :] = out[:, c * lanes : (c + 1) * lanes]
    for c in range(n_lane):
        ig_ref[:, c * lanes : (c + 1) * lanes] = xs[c].astype(BF16)
    outs[1].start()

    for d in range(1, n_sub):
        for c in range(n_col):
            z_send_all(d, c, lambda one: one.wait_send())
            q_copy(c, d, sub_id(d), me).wait_send()
        for turn in range(2):
            e_copy(turn, d, me).wait_send()
    for c in range(n_col):
        for halo in halo_pooled(c):
            halo.wait_send()
    for halo in halo_grad():
        halo.wait_send()
    for d in range(1, n_seq):
        a_copy(d, seq_id(d), s).wait_send()
    b_copy(0, s).wait_send()
    for d in range(1, n_chip):
        g_copy(d, s).wait_send()
        b_copy(d, 2 * lax.rem(chip + n_chip - d, n_chip) + core).wait_send()
    for out in outs:
        out.wait()


def hand_over_kernel(*refs):
    count = len(refs) // 2
    sems = refs[-1]
    moves = [pltpu.make_async_copy(refs[i], refs[count + i], sems.at[i]) for i in range(count)]
    for move in moves:
        move.start()
    for move in moves:
        move.wait()


def hand_over(*arrays):
    hbm = pl.BlockSpec(memory_space=pl.ANY)
    return pl.pallas_call(
        hand_over_kernel,
        out_shape=tuple(jax.ShapeDtypeStruct(a.shape, a.dtype) for a in arrays),
        in_specs=[hbm] * len(arrays),
        out_specs=(hbm,) * len(arrays),
        scratch_shapes=[pltpu.SemaphoreType.DMA((len(arrays),))],
    )(*arrays)


def per_device(activations, conv_weight, cotangent):
    n_seq, n_sub = lax.axis_size("seq"), lax.axis_size("sub")
    if not fits(activations, conv_weight, n_seq, n_sub):
        return per_device_plain(activations, conv_weight, cotangent)
    rows, in_width = activations.shape
    taps, ow, _ = conv_weight.shape
    own = rows // 4
    group = own * n_sub
    cs = in_width // n_seq
    n_chip = n_seq // 2
    n_col = 4
    width = in_width // n_col
    dma = pltpu.SemaphoreType.DMA
    hbm = pl.BlockSpec(memory_space=pl.ANY)
    far = pl.BlockSpec(memory_space=pltpu.HBM)
    features, input_grad, weight_grad = pl.pallas_call(
        functools.partial(kernel, n_seq, n_sub, taps),
        out_shape=(
            jax.ShapeDtypeStruct((ow, group), BF16),
            jax.ShapeDtypeStruct((rows, in_width), BF16),
            jax.ShapeDtypeStruct((taps, ow, cs), F32),
        ),
        in_specs=[far, far, far],
        out_specs=(hbm, hbm, hbm),
        scratch_shapes=[
            pltpu.VMEM((rows, in_width), BF16),
            pltpu.VMEM((taps * ow, in_width), BF16),
            pltpu.VMEM((ow, group), BF16),
            pltpu.VMEM((ow, group), BF16),
            pltpu.VMEM((rows, in_width), BF16),
            pltpu.VMEM((in_width // 128, rows, 128), F32),
            pltpu.VMEM((4, own, in_width), F32),
            pltpu.VMEM((4, own, in_width), F32),
            pltpu.VMEM((2, group + 2 * PAD, in_width), BF16),
            pltpu.VMEM((2, n_seq * group + 2 * PAD, cs), BF16),
            pltpu.VMEM((2, group + 2 * PAD, ow), BF16),
            pltpu.VMEM((n_seq, ow, 2 * group), BF16),
            pltpu.VMEM((2, n_sub, 8, 2 * group), F32),
            pltpu.VMEM((n_col, 2, group, width), BF16),
            pltpu.VMEM((n_sub, n_col, 2, own, width), BF16),
            pltpu.VMEM((taps, ow, cs), F32),
            dma((3,)), dma((3,)), dma((n_col, 2, n_sub)), dma((n_col, 2, n_sub)),
            dma((n_col, 2)), dma((n_col, 2)), dma((2,)), dma((2,)),
            dma((n_seq,)), dma((n_seq,)), dma, dma((2, n_sub)), dma((2, n_sub)),
            dma((n_chip,)), dma((n_chip,)), dma((n_chip,)), dma((n_chip,)),
            dma((n_col, n_sub)), dma((n_col, n_sub)),
        ],
        compiler_params=pltpu.CompilerParams(
            collective_id=0, has_side_effects=True, vmem_limit_bytes=VMEM_BYTES
        ),
        cost_estimate=pl.CostEstimate(
            flops=6 * 2 * group * taps * ow * in_width,
            bytes_accessed=2 * taps * ow * in_width,
            transcendentals=2 * rows * in_width,
        ),
    )(activations, conv_weight.reshape(taps * ow, in_width), cotangent.T)
    features, input_grad, weight_grad = hand_over(features, input_grad, weight_grad)
    return (features.T, input_grad, weight_grad.transpose(2, 0, 1))


def solution(mesh):
    return jax.shard_map(
        per_device,
        mesh=mesh,
        in_specs=(P(("seq", "sub"), None), P(None, "sub", None), P("seq", "sub")),
        out_specs=(P("seq", "sub"), P(("seq", "sub"), None), P("seq", None, "sub")),
        check_vma=False,
    )
```

```python
import functools

import jax
import jax.numpy as jnp
from jax import lax
from jax.experimental import pallas as pl
from jax.experimental.pallas import tpu as pltpu
from jax.sharding import PartitionSpec as P

EPSILON = 1e-06


def padded_2(block, sides, width):
    for axis, dim in sides:
        count = lax.axis_size(axis)
        forward = [(i, i + 1) for i in range(count - 1)]
        backward = [(target, source) for source, target in forward]
        low = lax.ppermute(
            lax.slice_in_dim(block, block.shape[dim] - width, None, axis=dim), axis, forward
        )
        high = lax.ppermute(lax.slice_in_dim(block, 0, width, axis=dim), axis, backward)
        block = jnp.concatenate([low, block, high], axis=dim)
    return block


def gelu_slope(tensor):
    return (
        0.5 * (1.0 + jax.scipy.special.erf(tensor * 0.7071067811865476))
        + tensor * jnp.exp(-0.5 * tensor * tensor) * 0.3989422804014327
    )


def pool_pairs(tensor):
    half_rows = tensor.shape[0] // 2
    return 0.5 * jnp.sum(tensor.reshape(half_rows, 2, tensor.shape[1]), axis=1)


def per_device_plain(activations, conv_weight, cotangent):
    tap_count = conv_weight.shape[0]
    in_width = activations.shape[1]
    out_width = conv_weight.shape[1]
    full_out = out_width * lax.axis_size("sub")
    x_float = activations.astype(jnp.float32)
    inv_first = lax.rsqrt(jnp.mean(x_float * x_float, axis=1, keepdims=True) + EPSILON)
    normed_first = x_float * inv_first
    pooled = pool_pairs(jax.nn.gelu(normed_first, approximate=False)).astype(jnp.bfloat16)
    gathered = lax.all_gather(pooled, "sub", axis=0, tiled=True)
    block_rows = gathered.shape[0]
    padded = padded_2(gathered, (("seq", 0),), 2)
    conv_acc = jnp.zeros((block_rows, out_width), jnp.float32)
    for offset in range(tap_count):
        conv_acc = conv_acc + lax.dot_general(
            padded[offset : offset + block_rows],
            conv_weight[offset],
            (((1,), (1,)), ((), ())),
            preferred_element_type=jnp.float32,
        )
    conv_out = conv_acc.astype(jnp.bfloat16)
    y_float = conv_out.astype(jnp.float32)
    square_sum = lax.psum(jnp.sum(y_float * y_float, axis=1), "sub")
    inv_second = lax.rsqrt(square_sum / full_out + EPSILON)[:, None]
    normed_second = y_float * inv_second
    features = pool_pairs(jax.nn.gelu(normed_second, approximate=False)).astype(jnp.bfloat16)
    upstream = 0.5 * jnp.repeat(cotangent.astype(jnp.float32), 2, axis=0)
    slope_second = upstream * gelu_slope(normed_second)
    inner_second = lax.psum(jnp.sum(slope_second * normed_second, axis=1), "sub")
    conv_grad = (
        inv_second * (slope_second - normed_second * (inner_second / full_out)[:, None])
    ).astype(jnp.bfloat16)
    grad_padded = padded_2(conv_grad, (("seq", 0),), 2)
    running = jnp.zeros((block_rows, in_width), jnp.float32)
    for offset in range(tap_count):
        window = lax.dynamic_slice_in_dim(grad_padded, 0 + 4 - offset, block_rows, 0)
        running = running + jnp.dot(window, conv_weight[offset], preferred_element_type=jnp.float32)
    owned = lax.psum_scatter(
        running.astype(jnp.bfloat16), "sub", scatter_dimension=1, tiled=True
    ).astype(jnp.float32)
    pooled_grad = lax.all_to_all(
        owned.astype(jnp.bfloat16), "sub", split_axis=0, concat_axis=1, tiled=True
    ).astype(owned.dtype)
    slope_first = 0.5 * jnp.repeat(pooled_grad, 2, axis=0) * gelu_slope(normed_first)
    inner_first = jnp.mean(slope_first * normed_first, axis=1, keepdims=True)
    input_grad = (inv_first * (slope_first - normed_first * inner_first)).astype(jnp.bfloat16)
    pieces = [
        lax.dot_general(
            padded[offset : offset + block_rows],
            conv_grad,
            (((0,), (0,)), ((), ())),
            preferred_element_type=jnp.float32,
        )
        for offset in range(tap_count)
    ]
    weight_grad = lax.psum_scatter(
        jnp.stack(pieces, axis=1).astype(jnp.bfloat16), "seq", scatter_dimension=0, tiled=True
    ).astype(jnp.float32)
    return (features, input_grad, weight_grad)


PAD = 16
VMEM_BYTES = 52 * 1024 * 1024
F32 = jnp.float32
BF16 = jnp.bfloat16


def gelu_half(tensor):
    return 0.5 * (1.0 + lax.erf(tensor * 0.7071067811865476))


def bell(tensor):
    return tensor * jnp.exp(-0.5 * tensor * tensor) * 0.3989422804014327


def fits(activations, conv_weight, n_seq, n_sub):
    rows, in_width = activations.shape
    group = rows * n_sub // 4
    return (
        n_seq % 2 == 0
        and in_width % (n_seq * 128) == 0
        and rows % 64 == 0
        and group % 128 == 0
        and conv_weight.shape[0] == 5
        and conv_weight.shape[1] % 16 == 0
        and n_seq * group <= 2048
    )


def kernel(
    n_seq, n_sub, taps,
    x_hbm, w_hbm, cot_hbm,
    feat_hbm, ig_hbm, wg_hbm,
    x_ref, w_ref, cot_ref, feat_ref, ig_ref, xs, n1, s1, p_ref, pa, gw, ga, sums, q_ref, r_ref, acc,
    in_sem, out_sem, z_send, z_recv, h_send, h_recv, k_send, k_recv, a_send, a_recv, a_loc, e_send, e_recv,
    g_send, g_recv, b_send, b_recv, q_send, q_recv,
):
    me = lax.axis_index("sub")
    s = lax.axis_index("seq")
    rows, in_width = x_ref.shape
    own = rows // 4
    group = own * n_sub
    ow = w_ref.shape[0] // taps
    full = ow * n_sub
    cs = in_width // n_seq
    n_chip = n_seq // 2
    chip, core = s // 2, s % 2
    n_col = q_send.shape[0]
    width = in_width // n_col

    def sub_id(d):
        return lax.rem(me + d, n_sub)

    def seq_id(d):
        return lax.rem(s + d, n_seq)

    def copy(src, dst, send, recv, **where):
        return pltpu.make_async_remote_copy(
            src_ref=src, dst_ref=dst, send_sem=send, recv_sem=recv,
            device_id=where, device_id_type=pl.DeviceIdType.MESH,
        )

    loads = [
        pltpu.make_async_copy(src, dst, in_sem.at[i])
        for i, (src, dst) in enumerate(((x_hbm, x_ref), (w_hbm, w_ref), (cot_hbm, cot_ref)))
    ]
    for load in loads:
        load.start()

    barrier = pltpu.get_barrier_semaphore()
    for d in range(1, n_sub):
        pl.semaphore_signal(barrier, inc=1, device_id={"sub": sub_id(d)}, device_id_type=pl.DeviceIdType.MESH)
    for d in range(1, n_seq):
        pl.semaphore_signal(barrier, inc=1, device_id={"seq": seq_id(d)}, device_id_type=pl.DeviceIdType.MESH)
    for side in (0, PAD + n_seq * group):
        pa[:, side : side + PAD, :] = jnp.zeros((2, PAD, cs), BF16)
    loads[0].wait()

    lanes = 128
    n_lane = in_width // lanes
    for c in range(n_lane):
        xs[c] = x_ref[:, c * lanes : (c + 1) * lanes].astype(F32)
    x_rows = [
        jnp.concatenate([xs[c, pl.ds(r, own, stride=4), :] for c in range(n_lane)], axis=1)
        for r in range(4)
    ]
    inv1 = [lax.rsqrt(jnp.mean(v * v, axis=1, keepdims=True) + EPSILON) for v in x_rows]
    mine = pl.ds(pl.multiple_of(PAD + own * me, 16), own)
    for parity in range(2):
        total = None
        for r in (2 * parity, 2 * parity + 1):
            v = x_rows[r] * inv1[r]
            half = gelu_half(v)
            n1[r] = v
            s1[r] = half
            total = v * half if total is None else total + v * half
        p_ref[parity, mine, :] = (0.5 * total).astype(BF16)

    pl.semaphore_wait(barrier, n_sub + n_seq - 2)

    def cols(c):
        return slice(c * width, (c + 1) * width)

    ways = ((1, n_sub - 1), (-1, 0))

    def z_copy(c, way, t, owner):
        step = ways[way][0]
        part = p_ref.at[:, pl.ds(pl.multiple_of(PAD + own * owner, 16), own), cols(c)]
        target = lax.rem(me + step + n_sub, n_sub)
        return copy(part, part, z_send.at[c, way, t - 1], z_recv.at[c, way, t - 1], sub=target)

    def has(way, t):
        return me >= t if way == 0 else me + t < n_sub

    def z_send_all(t, c, act):
        for way in range(2):
            step, last = ways[way]
            source = me - step * (t - 1)

            @pl.when(jnp.logical_and(has(way, t - 1), me != last))
            def _():
                act(z_copy(c, way, t, source))

    def z_wait(t, c):
        for way in range(2):
            step, last = ways[way]

            @pl.when(has(way, t))
            def _():
                z_copy(c, way, t, me - step * t).wait_recv()

    def z_start(t, c):
        z_send_all(t, c, lambda one: one.start())

    for c in range(n_col):
        z_start(1, c)
    for r in range(4):
        s1[r] += bell(n1[r])

    def up(ref, send, recv):
        return copy(ref.at[:, group : group + PAD, :], ref.at[:, 0:PAD, :], send, recv, seq=seq_id(1))

    def down(ref, send, recv):
        return copy(ref.at[:, PAD : 2 * PAD, :], ref.at[:, group + PAD : group + 2 * PAD, :],
                    send, recv, seq=seq_id(n_seq - 1))

    def halo_pooled(c):
        part = p_ref.at[:, :, cols(c)]
        return (up(part, h_send.at[c, 0], h_recv.at[c, 0]), down(part, h_send.at[c, 1], h_recv.at[c, 1]))

    def halo_grad():
        return (up(gw, k_send.at[0], k_recv.at[0]), down(gw, k_send.at[1], k_recv.at[1]))

    def shifts(v_e, v_o):
        return {
            (name, move): v[PAD + move : PAD + move + group]
            for name, v in (("e", v_e), ("o", v_o))
            for move in (-1, 0, 1)
        }

    def edges(v):
        low, middle, high = v[:, 0:PAD], v[:, PAD : PAD + group], v[:, PAD + group :]
        low = jnp.where(s == 0, jnp.zeros_like(low), low)
        high = jnp.where(s == n_seq - 1, jnp.zeros_like(high), high)
        return jnp.concatenate([low, middle, high], axis=1)

    even_taps = (("e", -1), ("o", -1), ("e", 0), ("o", 0), ("e", 1))
    odd_taps = (("o", -1), ("e", 0), ("o", 0), ("e", 1), ("o", 1))

    def tap_windows(win):
        return jnp.concatenate(
            [jnp.concatenate([win[even_taps[k]], win[odd_taps[k]]], axis=0) for k in range(taps)], axis=1)

    def conv_block(c):
        for halo in halo_pooled(c):
            halo.wait_recv()
        v = edges(p_ref[:, :, cols(c)])
        right = tap_windows(shifts(v[0], v[1]))
        left = jnp.concatenate([w_ref[k * ow : (k + 1) * ow, cols(c)] for k in range(taps)], axis=1)
        return lax.dot_general(left, right, (((1,), (1,)), ((), ())), preferred_element_type=F32)

    y = None
    for t in range(1, n_sub - 1):
        for c in range(n_col):
            z_wait(t, c)
            z_start(t + 1, c)
    for c in range(n_col):
        z_wait(n_sub - 1, c)
        for halo in halo_pooled(c):
            halo.start()
        if c == 0:
            loads[1].wait()
        else:
            term = conv_block(c - 1)
            y = term if y is None else y + term

    def a_part(block):
        return pa.at[:, pl.ds(pl.multiple_of(PAD + group * block, 16), group), :]

    def a_copy(d, slice_of, block):
        columns = pl.ds(pl.multiple_of(cs * slice_of, 128), cs)
        return copy(p_ref.at[:, PAD : PAD + group, columns], a_part(block),
                    a_send.at[d], a_recv.at[d], seq=seq_id(d))

    for d in range(1, n_seq):
        a_copy(d, seq_id(d), s).start()
    local = pltpu.make_async_copy(
        p_ref.at[:, PAD : PAD + group, pl.ds(pl.multiple_of(cs * s, 128), cs)], a_part(s), a_loc)
    local.start()
    y = y + conv_block(n_col - 1)
    y = y.astype(BF16).astype(F32)

    def e_copy(turn, d, owner):
        part = sums.at[turn, owner]
        return copy(part, part, e_send.at[turn, d], e_recv.at[turn, d], sub=sub_id(d))

    def reduce_start(turn, values):
        sums[turn, me] = jnp.broadcast_to(jnp.sum(values, axis=0, keepdims=True), (8, 2 * group))
        for d in range(1, n_sub):
            e_copy(turn, d, me).start()

    def reduce_end(turn):
        for d in range(1, n_sub):
            e_copy(turn, d, sub_id(n_sub - d)).wait_recv()
        total = sums[turn, 0]
        for j in range(1, n_sub):
            total = total + sums[turn, j]
        return total[0:1, :]

    reduce_start(0, y * y)
    loads[2].wait()
    cot = 0.5 * cot_ref[...].astype(F32)
    inv2 = lax.rsqrt(reduce_end(0) / full + EPSILON)
    v2 = y * inv2
    half = gelu_half(v2)
    slope = jnp.concatenate([cot, cot], axis=1) * (half + bell(v2))
    reduce_start(1, slope * v2)
    gelu2 = v2 * half
    feat_ref[...] = (0.5 * (gelu2[:, 0:group] + gelu2[:, group:])).astype(BF16)
    outs = [
        pltpu.make_async_copy(src, dst, out_sem.at[i])
        for i, (src, dst) in enumerate(((feat_ref, feat_hbm), (ig_ref, ig_hbm), (acc, wg_hbm)))
    ]
    outs[0].start()
    inner = reduce_end(1)
    grad = inv2 * (slope - v2 * (inner / full))
    turned = grad.T.astype(BF16)
    for parity in range(2):
        gw[parity, PAD : PAD + group, :] = turned[parity * group : (parity + 1) * group]
    for halo in halo_grad():
        halo.start()
    ga[s] = grad.astype(BF16)

    def g_copy(d, block):
        target = 2 * lax.rem(chip + d, n_chip) + core
        return copy(ga.at[block], ga.at[block], g_send.at[d], g_recv.at[d], seq=target)

    def b_copy(d, block):
        return copy(ga.at[block], ga.at[block], b_send.at[d], b_recv.at[d], seq=2 * chip + 1 - core)

    b_copy(0, s).start()
    for d in range(1, n_chip):
        g_copy(d, s).start()

    for halo in halo_grad():
        halo.wait_recv()
    v = edges(gw[...])
    win = shifts(v[0], v[1])
    even_back = (("e", 1), ("o", 0), ("e", 0), ("o", -1), ("e", -1))
    odd_back = (("o", 1), ("e", 1), ("o", 0), ("e", 0), ("o", -1))
    left = jnp.concatenate(
        [jnp.concatenate([win[even_back[k]], win[odd_back[k]]], axis=0) for k in range(taps)], axis=1)

    def q_copy(c, d, to, owner):
        return copy(
            q_ref.at[c, :, pl.ds(pl.multiple_of(own * to, 16), own), :],
            r_ref.at[owner, c],
            q_send.at[c, d], q_recv.at[c, d], sub=sub_id(d))

    for c in range(n_col):
        total = jnp.dot(left, w_ref[:, cols(c)], preferred_element_type=F32)
        q_ref[c] = total.astype(BF16).reshape(2, group, width)
        for d in range(1, n_sub):
            q_copy(c, d, sub_id(d), me).start()
        r_ref[me, c] = q_ref[c, :, pl.ds(pl.multiple_of(own * me, 16), own), :]

    for d in range(1, n_seq):
        a_copy(d, s, seq_id(n_seq - d)).wait_recv()
    local.wait()
    acc[...] = jnp.zeros_like(acc)

    def weight_block(block):
        base = pl.ds(pl.multiple_of(group * block, 16), group + 2 * PAD)
        right = tap_windows(shifts(pa[0, base, :], pa[1, base, :]))
        term = jnp.dot(ga[block], right, preferred_element_type=F32)
        for k in range(taps):
            acc[k] += term[:, k * cs : (k + 1) * cs]

    weight_block(s)

    def first_pass(d, carry):
        block = 2 * lax.rem(chip + n_chip - d, n_chip) + core
        g_copy(d, block).wait_recv()
        b_copy(d, block).start()
        weight_block(block)
        return carry

    def second_pass(d, carry):
        block = 2 * lax.rem(chip + n_chip - d, n_chip) + 1 - core
        b_copy(d, block).wait_recv()
        weight_block(block)
        return carry

    lax.fori_loop(1, n_chip, first_pass, 0)
    lax.fori_loop(0, n_chip, second_pass, 0)
    outs[2].start()

    pg = [[], []]
    for c in range(n_col):
        for d in range(1, n_sub):
            q_copy(c, d, me, sub_id(n_sub - d)).wait_recv()
        total = r_ref[0, c].astype(F32)
        for j in range(1, n_sub):
            total = total + r_ref[j, c].astype(F32)
        for parity in range(2):
            pg[parity].append(total[parity])
    pg = [jnp.concatenate(part, axis=1) for part in pg]
    for r in range(4):
        v = n1[r]
        slope1 = 0.5 * pg[r // 2] * s1[r]
        m1 = jnp.mean(slope1 * v, axis=1, keepdims=True)
        out = inv1[r] * (slope1 - v * m1)
        for c in range(n_lane):
            xs[c, pl.ds(r, own, stride=4), :] = out[:, c * lanes : (c + 1) * lanes]
    for c in range(n_lane):
        ig_ref[:, c * lanes : (c + 1) * lanes] = xs[c].astype(BF16)
    outs[1].start()

    for d in range(1, n_sub):
        for c in range(n_col):
            z_send_all(d, c, lambda one: one.wait_send())
            q_copy(c, d, sub_id(d), me).wait_send()
        for turn in range(2):
            e_copy(turn, d, me).wait_send()
    for c in range(n_col):
        for halo in halo_pooled(c):
            halo.wait_send()
    for halo in halo_grad():
        halo.wait_send()
    for d in range(1, n_seq):
        a_copy(d, seq_id(d), s).wait_send()
    b_copy(0, s).wait_send()
    for d in range(1, n_chip):
        g_copy(d, s).wait_send()
        b_copy(d, 2 * lax.rem(chip + n_chip - d, n_chip) + core).wait_send()
    for out in outs:
        out.wait()


def hand_over_kernel(*refs):
    count = len(refs) // 2
    sems = refs[-1]
    moves = [pltpu.make_async_copy(refs[i], refs[count + i], sems.at[i]) for i in range(count)]
    for move in moves:
        move.start()
    for move in moves:
        move.wait()


def hand_over(*arrays):
    hbm = pl.BlockSpec(memory_space=pl.ANY)
    return pl.pallas_call(
        hand_over_kernel,
        out_shape=tuple(jax.ShapeDtypeStruct(a.shape, a.dtype) for a in arrays),
        in_specs=[pl.BlockSpec(memory_space=pltpu.VMEM)] * len(arrays),
        out_specs=(hbm,) * len(arrays),
        scratch_shapes=[pltpu.SemaphoreType.DMA((len(arrays),))],
    )(*arrays)


def per_device(activations, conv_weight, cotangent):
    n_seq, n_sub = lax.axis_size("seq"), lax.axis_size("sub")
    if not fits(activations, conv_weight, n_seq, n_sub):
        return per_device_plain(activations, conv_weight, cotangent)
    rows, in_width = activations.shape
    taps, ow, _ = conv_weight.shape
    own = rows // 4
    group = own * n_sub
    cs = in_width // n_seq
    n_chip = n_seq // 2
    n_col = 4
    width = in_width // n_col
    dma = pltpu.SemaphoreType.DMA
    hbm = pl.BlockSpec(memory_space=pl.ANY)
    far = pl.BlockSpec(memory_space=pltpu.HBM)
    features, input_grad, weight_grad = pl.pallas_call(
        functools.partial(kernel, n_seq, n_sub, taps),
        out_shape=(
            jax.ShapeDtypeStruct((ow, group), BF16),
            jax.ShapeDtypeStruct((rows, in_width), BF16),
            jax.ShapeDtypeStruct((taps, ow, cs), F32),
        ),
        in_specs=[far, far, far],
        out_specs=(hbm, hbm, hbm),
        scratch_shapes=[
            pltpu.VMEM((rows, in_width), BF16),
            pltpu.VMEM((taps * ow, in_width), BF16),
            pltpu.VMEM((ow, group), BF16),
            pltpu.VMEM((ow, group), BF16),
            pltpu.VMEM((rows, in_width), BF16),
            pltpu.VMEM((in_width // 128, rows, 128), F32),
            pltpu.VMEM((4, own, in_width), F32),
            pltpu.VMEM((4, own, in_width), F32),
            pltpu.VMEM((2, group + 2 * PAD, in_width), BF16),
            pltpu.VMEM((2, n_seq * group + 2 * PAD, cs), BF16),
            pltpu.VMEM((2, group + 2 * PAD, ow), BF16),
            pltpu.VMEM((n_seq, ow, 2 * group), BF16),
            pltpu.VMEM((2, n_sub, 8, 2 * group), F32),
            pltpu.VMEM((n_col, 2, group, width), BF16),
            pltpu.VMEM((n_sub, n_col, 2, own, width), BF16),
            pltpu.VMEM((taps, ow, cs), F32),
            dma((3,)), dma((3,)), dma((n_col, 2, n_sub)), dma((n_col, 2, n_sub)),
            dma((n_col, 2)), dma((n_col, 2)), dma((2,)), dma((2,)),
            dma((n_seq,)), dma((n_seq,)), dma, dma((2, n_sub)), dma((2, n_sub)),
            dma((n_chip,)), dma((n_chip,)), dma((n_chip,)), dma((n_chip,)),
            dma((n_col, n_sub)), dma((n_col, n_sub)),
        ],
        compiler_params=pltpu.CompilerParams(
            collective_id=0, has_side_effects=True, vmem_limit_bytes=VMEM_BYTES
        ),
        cost_estimate=pl.CostEstimate(
            flops=6 * 2 * group * taps * ow * in_width,
            bytes_accessed=2 * taps * ow * in_width,
            transcendentals=2 * rows * in_width,
        ),
    )(activations, conv_weight.reshape(taps * ow, in_width), cotangent.T)
    features, input_grad, weight_grad = hand_over(features, input_grad, weight_grad)
    return (features.T, input_grad, weight_grad.transpose(2, 0, 1))


def solution(mesh):
    return jax.shard_map(
        per_device,
        mesh=mesh,
        in_specs=(P(("seq", "sub"), None), P(None, "sub", None), P("seq", "sub")),
        out_specs=(P("seq", "sub"), P(("seq", "sub"), None), P("seq", None, "sub")),
        check_vma=False,
    )
```
